256 devices in a mesh: depth: 4 (over x), gx: 16 (over z, core), gy: 4 (over y).
Axes of the slice: x: 4, y: 4, z: 8, core: 2. Of those that a mesh axis runs over, the one named last changes fastest.
Arguments:
- density: float32 [16, 512, 1024], P('depth', 'gx', 'gy'), may hold values from 0.1 to 1
- table_index: int32 [16, 512, 1024], P('depth', 'gx', 'gy'), may hold values from 0 to 255
- opacity_table: float32 [256], replicated, may hold values from 0.02 to 0.3
- color_table: float32 [3, 256], replicated, may hold values from 0.5 to 3
- light_direction: float32 [4, 3], replicated, may hold values from -4 to 4
- shear_offsets: int32 [4, 16, 2], replicated, may hold values from -16 to 16, as said below
Outputs:
- image: float32 [4, 4, 512, 1024], P('depth', None, 'gx', 'gy')
The draws below stay inside these ranges and needn't reach their ends.
Inputs may be any that keep to these rules, and one draw needn't show every extreme that they name: `shear_offsets`: every offset lies within -16 to 16; both ends occur in every draw.
All inputs are finite; a program needn't handle non-finite values.
Results may differ from the reference program's by a relative error of at most 0.000051.
Values sent between devices are 32-bit elements; how exact they have to be, the bound alone decides.
No kernel may reach another device: no remote copies, remote signals or barrier semaphores. Data moves between devices by JAX's collectives and lax.ppermute only.
A program may use at most 64 MiB of HBM per device.

```python
import math
import jax
import jax.numpy as jnp
from jax import lax

LUT = 256
VIEWS = 4
MAXS = 16
NZ = 16
NX = 512
NY = 1024


def draw_shear_offsets(key, part):
    offsets = jax.random.randint(key, (VIEWS, NZ, 2), -MAXS, MAXS + 1)
    offsets = offsets.at[0, 0, 0].set(MAXS)
    offsets = offsets.at[VIEWS - 1, NZ - 1, 1].set(-MAXS)
    return offsets.astype(jnp.int32)


def plant(array, rng, least, high):
    place = [jax.random.randint(jax.random.fold_in(rng, axis), (), 0, length) for axis, length in enumerate(array.shape)]
    widest = array.shape.index(max(array.shape))
    neighbour = place[:widest] + [(place[widest] + 1) % array.shape[widest]] + place[widest + 1:]
    return array.at[tuple(place)].set(least).at[tuple(neighbour)].set(high)


def level_of(own_key, dims, split, low, high):
    def one(dim, parts):
        draws = jax.random.uniform(jax.random.fold_in(jax.random.fold_in(own_key, 6), dim), (parts,), jnp.float32, low / len(split), high / len(split))
        return jnp.repeat(jnp.exp(draws), dims[dim] // parts).reshape((-1,) + (1,) * (len(dims) - dim - 1))

    level = one(*split[0])
    for cut in split[1:]:
        level = level * one(*cut)
    return level


def scatter_about(own_key, dims, width, most, held_as=jnp.bfloat16):
    entries = jax.random.normal(own_key, dims, jnp.float32) * width
    return jnp.minimum(jnp.maximum(entries, -most), most).astype(held_as)


def setup_inputs(seed: int = 0) -> dict:
    keys = jax.random.split(jax.random.key(seed), 7)
    return {
        "density": jnp.clip(0.1 + 0.9 * jax.random.uniform(keys[0], (NZ, NX, NY), jnp.float32) ** level_of(keys[0], (NZ, NX, NY), ((0, 4), (1, 16), (2, 4)), -0.2, 0.2), 0.1, 1.0),
        "table_index": plant(jax.random.randint(keys[1], (NZ, NX, NY), 0, LUT), jax.random.fold_in(keys[1], 1), 0, LUT - 1).astype(jnp.int32),
        "opacity_table": jnp.clip(jnp.exp(jax.random.uniform(keys[2], (LUT,), jnp.float32, math.log(0.02), math.log(0.3))), 0.02, 0.3),
        "color_table": jnp.clip(jax.random.uniform(keys[3], (3, LUT), jnp.float32, 0.5, 3.0), 0.5, 3.0),
        "light_direction": scatter_about(keys[4], (VIEWS, 3), 1.0, 4.0, jnp.float32),
        "shear_offsets": draw_shear_offsets(jax.random.fold_in(keys[6], 71), 0),
    }


ambient = 0.3
diffuse = 0.7

def reference(density, table_index, opacity_table, color_table, light_direction, shear_offsets):
    padded = jnp.pad(density, 1)
    accums = [jnp.zeros((4, NX, NY), jnp.float32) for view in range(VIEWS)]
    for depth_pos in range(NZ):
        center = padded[depth_pos + 1]
        slope_depth = 0.5 * (padded[depth_pos + 2, 1:-1, 1:-1] - padded[depth_pos, 1:-1, 1:-1])
        slope_row = 0.5 * (center[2:, 1:-1] - center[:-2, 1:-1])
        slope_col = 0.5 * (center[1:-1, 2:] - center[1:-1, :-2])
        inner = center[1:-1, 1:-1]
        index_slice = table_index[depth_pos]
        kappa = opacity_table[index_slice]
        colors = color_table[:, index_slice]
        alpha = 1.0 - jnp.exp(-kappa * inner)
        base = alpha[None] * colors
        lengths = jnp.sqrt(slope_depth * slope_depth + slope_row * slope_row + slope_col * slope_col + 1.0)
        for view in range(VIEWS):
            light = light_direction[view]
            lambert = jnp.abs(light[0] * slope_depth + light[1] * slope_row + light[2] * slope_col) / lengths
            fragment = jnp.concatenate([alpha[None], base * (ambient + diffuse * lambert)[None]], axis=0)
            framed = jnp.pad(fragment, ((0, 0), (MAXS, MAXS), (MAXS, MAXS)))
            start_row = (MAXS - shear_offsets[view, depth_pos, 0]).astype(jnp.int32)
            start_col = (MAXS - shear_offsets[view, depth_pos, 1]).astype(jnp.int32)
            shifted = lax.dynamic_slice(framed, (jnp.int32(0), start_row, start_col), (4, NX, NY))
            accums[view] = accums[view] + (1.0 - accums[view][0:1]) * shifted
    return jnp.stack(accums)
```

```python
import functools

import jax
import jax.numpy as jnp
from jax import lax
from jax.experimental import pallas as pl
from jax.experimental.pallas import tpu as pltpu
from jax.sharding import PartitionSpec as P

VIEWS = 4
MAXS = 16
SLICES = 4
ROWS = 32
COLS = 256
LANES = 128
EXT = ROWS + 2 * MAXS
FRAME = EXT + 16

ambient = 0.3
diffuse = 0.7

VMEM = pl.BlockSpec(memory_space=pltpu.VMEM)
SMEM = pl.BlockSpec(memory_space=pltpu.SMEM)
PARAMS = pltpu.CompilerParams(vmem_limit_bytes=32 * 1024 * 1024)


def f32(*shape):
    return jax.ShapeDtypeStruct(shape, jnp.float32)


def roll(value, shift):
    shift = shift % LANES
    return pltpu.roll(value, shift, 1) if shift else value


def lane_iota(rows):
    return lax.broadcasted_iota(jnp.int32, (rows, LANES), 1)


def pack_rows(density, index, last, first):
    for target, start, extra in ((last, ROWS - MAXS, ROWS - MAXS - 1), (first, 0, MAXS)):
        for s in range(SLICES):
            target[MAXS * s : MAXS * (s + 1)] = density[s, start : start + MAXS]
            target[EXT + MAXS * s : EXT + MAXS * (s + 1)] = index[s, start : start + MAXS].astype(
                jnp.float32
            )
        target[2 * EXT :] = jnp.zeros((8, COLS), jnp.float32)
        for s in range(SLICES):
            target[2 * EXT + s : 2 * EXT + s + 1] = density[s, extra : extra + 1]


def inside(axis):
    place = lax.axis_index(axis)
    return place > 0, place < lax.axis_size(axis) - 1


def tall(own, top, bottom, plane, keep, lanes):
    above = top[MAXS * plane : MAXS * (plane + 1), lanes]
    below = bottom[MAXS * plane : MAXS * (plane + 1), lanes]
    if keep is not None:
        above = jnp.where(keep[0], above, 0.0)
        below = jnp.where(keep[1], below, 0.0)
    return jnp.concatenate([above, own, below], axis=0)


def outer_rows(top, bottom, s, keep, lanes):
    above = jnp.where(keep[0], top[2 * EXT + s : 2 * EXT + s + 1, lanes], 0.0)
    below = jnp.where(keep[1], bottom[2 * EXT + s : 2 * EXT + s + 1, lanes], 0.0)
    sub = lax.broadcasted_iota(jnp.int32, (8, LANES), 0)
    return jnp.where(sub == 7, above, below)


def pack_cols(density, index, top, bottom, last, first):
    keep = inside("gx")
    lane = lane_iota(8)
    for target, lanes, turn, edge in (
        (last, slice(LANES, 2 * LANES), MAXS, LANES - MAXS - 1),
        (first, slice(0, LANES), 0, MAXS),
    ):
        main = [jnp.zeros((8, LANES), jnp.float32) for _ in range(9)]
        outer = [jnp.zeros((8, LANES), jnp.float32) for _ in range(2)]
        for plane in range(2 * SLICES):
            s = plane % SLICES
            if plane < SLICES:
                block = tall(density[s, :, lanes], top, bottom, plane, keep, lanes)
                block = jnp.concatenate([block, outer_rows(top, bottom, s, keep, lanes)], axis=0)
            else:
                block = tall(index[s, :, lanes].astype(jnp.float32), top, bottom, plane, None, lanes)
            mine = (lane >= MAXS * plane) & (lane < MAXS * (plane + 1))
            for t in range(block.shape[0] // 8):
                main[t] = jnp.where(mine, roll(block[8 * t : 8 * t + 8], MAXS * plane + turn), main[t])
            if plane < SLICES:
                for t in range(8):
                    shift = MAXS * plane + turn + t // 2
                    here = lane == (edge + shift) % LANES
                    outer[t % 2] = jnp.where(here, roll(block[8 * t : 8 * t + 8], shift), outer[t % 2])
        for t, value in enumerate(main + outer):
            target[8 * t : 8 * t + 8] = value


def assemble(density, index, top, bottom, left, right, frame, codes, first, last):
    keep = inside("gx")
    keep_left, keep_right = inside("gy")
    lane = lane_iota(8)
    from_left = lane >= LANES - MAXS - 1
    for s in range(SLICES):
        for k in range(2):
            lanes = slice(LANES * k, LANES * (k + 1))
            frame[s, k, 8 : 8 + EXT] = tall(density[s, :, lanes], top, bottom, s, keep, lanes)
            ends = outer_rows(top, bottom, s, keep, lanes)
            frame[s, k, 0:8] = ends
            frame[s, k, 8 + EXT :] = ends
            codes[s, k] = tall(
                index[s, :, lanes].astype(jnp.float32), top, bottom, SLICES + s, None, lanes
            ).astype(jnp.int32)
        for t in range(9):
            rows = slice(8 * t, 8 * t + 8)
            low = roll(left[rows], LANES - MAXS - MAXS * s)
            high = roll(right[rows], -MAXS * s)
            if t < 8:
                rest = slice(72 + 8 * (t % 2), 80 + 8 * (t % 2))
                outer = roll(left[rest], LANES - MAXS - MAXS * s - t // 2)
                low = jnp.where(lane == LANES - MAXS - 1, outer, low)
                outer = roll(right[rest], -MAXS * s - t // 2)
                high = jnp.where(lane == MAXS, outer, high)
            low = jnp.where(keep_left & from_left, low, 0.0)
            side = jnp.where(keep_right & (lane <= MAXS), high, low)
            if t < 8:
                frame[s, 2, 8 + 8 * t : 16 + 8 * t] = side
                low = roll(left[rows], LANES - MAXS - MAXS * (SLICES + s))
                high = roll(right[rows], -MAXS * (SLICES + s))
                value = jnp.where(lane < MAXS, high, jnp.where(from_left, low, 0.0))
                codes[s, 2, rows] = value.astype(jnp.int32)
            else:
                frame[s, 2, 0:8] = side
                frame[s, 2, 8 + EXT :] = side
    first[...] = frame[0, :, 8 : 8 + EXT]
    last[...] = frame[SLICES - 1, :, 8 : 8 + EXT]


def look_up(tables, code):
    low = code & (LANES - 1)
    under = code < LANES
    values = []
    for c in range(4):
        halves = [
            jnp.take_along_axis(
                jnp.broadcast_to(tables[c : c + 1, LANES * h : LANES * (h + 1)], code.shape),
                low,
                axis=1,
                mode="promise_in_bounds",
            )
            for h in range(2)
        ]
        values.append(jnp.where(under, *halves))
    return values


def shade(frame, codes, before, after, opacity, colors, light, shear, *refs):
    images, (scaled, alphas, bases) = refs[:VIEWS], refs[VIEWS:]
    depth_pos = lax.axis_index("depth")
    keep_before, keep_after = inside("depth")
    tables = jnp.concatenate([opacity[...], colors[...]], axis=0)
    lane = lane_iota(8)
    for s in range(SLICES):

        def row_tile(t, carry, s=s):
            at = pl.multiple_of(8 * t, 8)
            here = [frame[s, k, pl.ds(at + 8, 8)] for k in range(3)]
            to_right = [roll(value, 1) for value in here]
            to_left = [roll(value, -1) for value in here]
            for k in range(3):
                rows = (k, pl.ds(at, 8))
                if s == 0:
                    front = jnp.where(keep_before, before[rows], 0.0)
                else:
                    front = frame[s - 1, k, pl.ds(at + 8, 8)]
                if s == SLICES - 1:
                    back = jnp.where(keep_after, after[rows], 0.0)
                else:
                    back = frame[s + 1, k, pl.ds(at + 8, 8)]
                slope_depth = 0.5 * (back - front)
                slope_row = 0.5 * (
                    frame[s, k, pl.ds(at + 9, 8)] - frame[s, k, pl.ds(at + 7, 8)]
                )
                before_col = jnp.where(lane == 0, to_right[k - 1], to_right[k])
                after_col = jnp.where(lane == LANES - 1, to_left[(k + 1) % 3], to_left[k])
                slope_col = 0.5 * (after_col - before_col)
                scale = diffuse * lax.rsqrt(
                    slope_depth * slope_depth + slope_row * slope_row + slope_col * slope_col + 1.0
                )
                scaled[s, 0, *rows] = slope_depth * scale
                scaled[s, 1, *rows] = slope_row * scale
                scaled[s, 2, *rows] = slope_col * scale
                kappa, *color = look_up(tables, codes[s, *rows])
                alpha = 1.0 - jnp.exp(-kappa * here[k])
                alphas[s, *rows] = alpha
                for c in range(3):
                    bases[s, c, *rows] = alpha * color[c]
            return carry

        lax.fori_loop(0, EXT // 8, row_tile, 0)

    for k in range(VIEWS):
        view = depth_pos ^ k
        image = images[k]
        lights = [light[view, c] for c in range(3)]

        def row_tile(t, carry, view=view, image=image, lights=lights):
            accum = [[jnp.zeros((8, LANES), jnp.float32)] * 2 for _ in range(4)]
            for s in range(SLICES):
                shift_row = shear[view, depth_pos * SLICES + s, 0]
                shift_col = shear[view, depth_pos * SLICES + s, 1]
                turn = jnp.where(shift_col < 0, shift_col + LANES, shift_col)
                low = lane < shift_col
                high = lane > shift_col + (LANES - 1)
                start = 8 * t + MAXS - shift_row
                channels = [[], [], [], []]
                for j in range(3):
                    rows = (j, pl.ds(start, 8))
                    gain = ambient + jnp.abs(
                        lights[0] * scaled[s, 0, *rows]
                        + lights[1] * scaled[s, 1, *rows]
                        + lights[2] * scaled[s, 2, *rows]
                    )
                    channels[0].append(pltpu.roll(alphas[s, *rows], turn, 1))
                    for c in range(3):
                        channels[c + 1].append(pltpu.roll(bases[s, c, *rows] * gain, turn, 1))
                moved = [
                    (
                        jnp.where(low, r2, jnp.where(high, r1, r0)),
                        jnp.where(low, r0, jnp.where(high, r2, r1)),
                    )
                    for r0, r1, r2 in channels
                ]
                clear = [1.0 - accum[0][h] for h in range(2)]
                accum = [
                    [accum[c][h] + clear[h] * moved[c][h] for h in range(2)] for c in range(4)
                ]
            rows = pl.ds(pl.multiple_of(8 * t, 8), 8)
            for c in range(4):
                for h in range(2):
                    image[c, rows, LANES * h : LANES * (h + 1)] = accum[c][h]
            return carry

        lax.fori_loop(0, ROWS // 8, row_tile, 0)


def merge(own, one, two, three, out):
    depth_pos = lax.axis_index("depth")
    odd = depth_pos % 2 == 1
    high = depth_pos >= 2

    def row_tile(t, carry):
        rows = pl.ds(pl.multiple_of(8 * t, 8), 8)

        def over(flip, near, far):
            front = [jnp.where(flip, b, a) for a, b in zip(near, far)]
            back = [jnp.where(flip, a, b) for a, b in zip(near, far)]
            clear = 1.0 - front[0]
            return [a + clear * b for a, b in zip(front, back)]

        for h in range(2):
            lanes = slice(LANES * h, LANES * (h + 1))
            parts = [[ref[c, rows, lanes] for c in range(4)] for ref in (own, one, two, three)]
            total = over(high, over(odd, parts[0], parts[1]), over(odd, parts[2], parts[3]))
            for c in range(4):
                out[0, c, rows, lanes] = total[c]
        return carry

    lax.fori_loop(0, ROWS // 8, row_tile, 0)


def call(kernel, ins, outs, scratch=(), cost=1000000):
    return pl.pallas_call(
        kernel,
        out_shape=outs,
        in_specs=ins,
        out_specs=[VMEM] * len(outs),
        scratch_shapes=scratch,
        compiler_params=PARAMS,
        cost_estimate=pl.CostEstimate(flops=cost, bytes_accessed=cost, transcendentals=0),
    )


def neighbours(to_next, to_previous, axis):
    count = lax.axis_size(axis)
    ahead = [(i, (i + 1) % count) for i in range(count)]
    return (
        lax.ppermute(to_next, axis, ahead),
        lax.ppermute(to_previous, axis, [(target, source) for source, target in ahead]),
    )


def local(density, table_index, opacity_table, color_table, light_direction, shear_offsets):
    strip = f32(2 * EXT + 8, COLS)
    last, first = call(pack_rows, [VMEM] * 2, [strip, strip])(density, table_index)
    top, bottom = neighbours(last, first, "gx")
    strip = f32(88, LANES)
    last, first = call(pack_cols, [VMEM] * 4, [strip, strip])(density, table_index, top, bottom)
    left, right = neighbours(last, first, "gy")
    frame, codes, first, last = call(
        assemble,
        [VMEM] * 6,
        [
            f32(SLICES, 3, FRAME, LANES),
            jax.ShapeDtypeStruct((SLICES, 3, EXT, LANES), jnp.int32),
            f32(3, EXT, LANES),
            f32(3, EXT, LANES),
        ],
    )(density, table_index, top, bottom, left, right)
    before, after = neighbours(last, first, "depth")
    images = call(
        shade,
        [VMEM] * 6 + [SMEM] * 2,
        [f32(4, ROWS, COLS)] * VIEWS,
        [
            pltpu.VMEM((SLICES, 3, 3, EXT, LANES), jnp.float32),
            pltpu.VMEM((SLICES, 3, EXT, LANES), jnp.float32),
            pltpu.VMEM((SLICES, 3, 3, EXT, LANES), jnp.float32),
        ],
    )(
        frame,
        codes,
        before,
        after,
        opacity_table[None],
        color_table,
        light_direction,
        shear_offsets,
    )
    received = [images[0]]
    for k in (1, 2, 3):
        received.append(lax.ppermute(images[k], "depth", [(i, i ^ k) for i in range(4)]))
    return call(merge, [VMEM] * 4, [f32(1, 4, ROWS, COLS)])(*received)[0]


def solution(mesh):
    return jax.shard_map(
        local,
        mesh=mesh,
        in_specs=(P("depth", "gx", "gy"), P("depth", "gx", "gy"), P(), P(), P(), P()),
        out_specs=P("depth", None, "gx", "gy"),
        check_vma=False,
    )
```
